32 devices in a mesh: rep: 4 (over z), gx: 4 (over x, core), gy: 2 (over y).
Axes of the slice: x: 2, y: 2, z: 4, core: 2. Of those that a mesh axis runs over, the one named last changes fastest.
Arguments:
- velocity: bfloat16 [4, 128, 64, 128], P('rep', 'gx', 'gy'), may hold values from -1.5 to 1.5
- tracers: bfloat16 [4, 128, 64, 128], P('rep', 'gx', 'gy'), may hold values from 0.5 to 2
- forcing: bfloat16 [12, 128, 64, 128], P('rep', 'gx', 'gy'), may hold values from -6 to 6
- coefficients: float32 [12], P('rep'), may hold values from -1.2 to 1.2
- land_mask: int32 [128, 64], P('gx', 'gy'), may hold values 0 or 1
- step_levels: int32 [3], replicated, may hold values from 0 to 3
Outputs:
- combined: float32 [128, 64, 128], P(('gx', 'rep'), 'gy')
- adjoints: float32 [12, 128, 64, 128], P('rep', 'gx', 'gy')
The draws below stay inside these ranges and needn't reach their ends.
Inputs may be any that keep to these rules, and one draw needn't show every extreme that they name: `step_levels`: each entry names the group along rep that stores the level.
All inputs are finite; a program needn't handle non-finite values. No bound on the sum of `land_mask` on one device may be relied on, other than what follows from the above.
Results may differ from the reference program's by a relative error of at most 0.0003.
Values may be sent and summed in bfloat16 or wider, within the bound.
A program may use at most 64 MiB of HBM per device.

```python
import math
import jax
import jax.numpy as jnp
from jax import lax

NZ = 64
STEPS = 3
REPS = 12
NX = 128
NY = 64
LEVELS = 4
N_REP = 4


def set_ends(values, own_key, smallest, largest):
    extent = values.shape
    place = [jax.random.randint(jax.random.fold_in(own_key, axis), (), 0, extent[axis]) for axis in range(len(extent))]
    values = values.at[tuple(place)].set(smallest)
    longest = extent.index(max(extent))
    place[longest] = (place[longest] + 1) % extent[longest]
    return values.at[tuple(place)].set(largest)


def steps_of(own_key, extent, shards, low, largest):
    gain, own = 1.0, jax.random.fold_in(own_key, 6)
    for position, blocks in shards:
        steps = jnp.exp(jax.random.uniform(jax.random.fold_in(own, position), (blocks,), jnp.float32, low / len(shards), largest / len(shards)))
        gain = gain * jnp.repeat(steps, extent[position] // blocks).reshape([-1 if axis == position else 1 for axis in range(len(extent))])
    return gain


def gaussian(rng, dims, scale, bound, split=(), held_as=jnp.bfloat16):
    drawn = scale * jax.random.normal(rng, dims, jnp.float32)
    if split:
        drawn = drawn * steps_of(rng, dims, split, -0.22, 0.18)
    return jnp.clip(drawn, -bound, bound).astype(held_as)


def setup_inputs(seed: int = 0) -> dict:
    splits = jax.random.split(jax.random.key(seed), 7)
    velocity = jnp.clip(jax.random.uniform(splits[0], (LEVELS, NX, NY, 2 * NZ), jnp.float32, -1.5, 1.5) * steps_of(splits[0], (LEVELS, NX, NY, 2 * NZ), ((0, 4), (1, 4), (2, 2)), -0.4, 0.0), -1.5, 1.5).astype(jnp.bfloat16)
    tracers = jnp.clip(jnp.exp(math.log(2.0) - 1.3862944 * jax.random.uniform(splits[1], (LEVELS, NX, NY, 2 * NZ), jnp.float32) ** steps_of(splits[1], (LEVELS, NX, NY, 2 * NZ), ((0, 4), (1, 4), (2, 2)), -0.2, 0.2)), 0.5, 2.0).astype(jnp.bfloat16)
    forcing = gaussian(splits[2], (REPS, NX, NY, 2 * NZ), 1.0, 6.0, ((0, 4), (1, 4), (2, 2)))
    coefficients = gaussian(splits[3], (REPS,), 0.2, 1.2, ((0, 4),), jnp.float32)
    land_mask = set_ends((jax.random.randint(splits[4], (NX, NY), 0, 8) < 7).astype(jnp.int32), jax.random.fold_in(splits[4], 1), 0, 1)
    step_levels = jax.random.randint(splits[5], (STEPS,), 0, N_REP).astype(jnp.int32)
    return {"velocity": velocity, "tracers": tracers, "forcing": forcing, "coefficients": coefficients, "land_mask": land_mask, "step_levels": step_levels}


time_step = 0.1


def advance(state, speed, tracer, ocean):
    half = state.shape[-1] // 2
    along_x = jnp.concatenate([speed[..., :half], speed[..., :half]], axis=-1)
    along_y = jnp.concatenate([speed[..., half:], speed[..., half:]], axis=-1)
    east = jnp.pad(along_x * state, ((1, 1), (1, 1), (0, 0)))
    north = jnp.pad(along_y * state, ((1, 1), (1, 1), (0, 0)))
    padded = jnp.pad(state, ((1, 1), (1, 1), (0, 0)))
    advect = 0.5 * (east[:-2, 1:-1] - east[2:, 1:-1]) + 0.5 * (north[1:-1, :-2] - north[1:-1, 2:])
    spread = padded[:-2, 1:-1] + padded[2:, 1:-1] + padded[1:-1, :-2] + padded[1:-1, 2:] - 4.0 * state
    mixing = tracer[..., :half] * state[..., :half] - tracer[..., half:] * state[..., half:]
    exchange = jnp.concatenate([-mixing, mixing], axis=-1)
    return ocean * (state + time_step * (advect + spread + exchange))


def reference(velocity, tracers, forcing, coefficients, land_mask, step_levels):
    ocean = land_mask.astype(jnp.float32)[:, :, None]
    speeds = velocity[step_levels].astype(jnp.float32)
    tracer_levels = tracers[step_levels].astype(jnp.float32)

    def one(total, item):
        force, weight = item
        state = force.astype(jnp.float32)
        for step in range(STEPS):
            state = advance(state, speeds[step], tracer_levels[step], ocean)
        return total + weight * state, state

    start = jnp.zeros(forcing.shape[1:], jnp.float32)
    total, adjoints = lax.scan(one, start, (forcing, coefficients))
    return total, adjoints
```

```python
import functools

import jax
import jax.numpy as jnp
from jax import lax
from jax.experimental import pallas as pl
from jax.experimental.pallas import tpu as pltpu
from jax.sharding import PartitionSpec as P

MESH = pl.DeviceIdType.MESH
STEPS = 3
F32 = jnp.float32
time_step = 0.1


def kernel(
    sizes, pieces, ahead,
    vel, tra, forcing, coef, mask, levels,
    comb, adj,
    states, up, dn, cu, cv, ct, ocean, wsum, rs_up, rs_dn, xs, xr, ys, yr,
    up_s, up_r, dn_s, dn_r, xs_s, xs_r, ys_s, ys_r, rs_s, rs_r,
):
    n, nx, ny = sizes
    reps, rows, cols, lanes = forcing.shape
    half = lanes // 2
    per = rows // pieces
    share = rows // n
    unit = min(per, share)
    z, x, y = lax.axis_index("rep"), lax.axis_index("gx"), lax.axis_index("gy")

    barrier = pltpu.get_barrier_semaphore()
    links = (("rep", z, n), ("gx", x, nx), ("gy", y, ny))
    for name, at, count in links:
        @pl.when(at > 0)
        def _():
            pl.semaphore_signal(barrier, inc=1, device_id={name: at - 1}, device_id_type=MESH)

        @pl.when(at < count - 1)
        def _():
            pl.semaphore_signal(barrier, inc=1, device_id={name: at + 1}, device_id_type=MESH)

    lane = lax.broadcasted_iota(jnp.int32, (cols, lanes), 1)
    row_of = lax.broadcasted_iota(jnp.int32, (cols, lanes), 0)
    first = lane < half
    eye = lax.broadcasted_iota(jnp.int32, (cols, cols), 0) == lax.broadcasted_iota(jnp.int32, (cols, cols), 1)

    def fill_ocean():
        for r in range(rows):
            line = jnp.where(eye, mask[r : r + 1, :].astype(F32), 0.0)
            ocean[r] = jnp.broadcast_to(jnp.sum(line, axis=1, keepdims=True), (cols, lanes))

    def fill_ends():
        none = jnp.zeros(xr.shape[2:], F32)
        thin = jnp.zeros(yr.shape[2:], F32)
        for k in range(STEPS):
            for side, at, count in ((0, x, 0), (1, x, nx - 1)):
                @pl.when(at == count)
                def _():
                    xr[k, side] = none
            for side, at, count in ((0, y, 0), (1, y, ny - 1)):
                @pl.when(at == count)
                def _():
                    yr[k, side] = thin

    def up_copy(k, c):
        part = up.at[k, pl.ds(c * per, per)]
        return pltpu.make_async_remote_copy(part, part, up_s.at[k, c], up_r.at[k, c], {"rep": jnp.minimum(z + 1, n - 1)}, MESH)

    def dn_copy(k, c):
        part = dn.at[k, pl.ds(c * per, per)]
        return pltpu.make_async_remote_copy(part, part, dn_s.at[k, c], dn_r.at[k, c], {"rep": jnp.maximum(z - 1, 0)}, MESH)

    def x_copy(k, side):
        to = jnp.minimum(x + 1, nx - 1) if side == 0 else jnp.maximum(x - 1, 0)
        return pltpu.make_async_remote_copy(
            xs.at[k, side], xr.at[k, side], xs_s.at[k, side], xs_r.at[k, side], {"gx": to}, MESH)

    def y_copy(k, side, c):
        to = jnp.minimum(y + 1, ny - 1) if side == 0 else jnp.maximum(y - 1, 0)
        part = pl.ds(c * per, per)
        return pltpu.make_async_remote_copy(
            ys.at[k, side, part], yr.at[k, side, part], ys_s.at[k, side, c], ys_r.at[k, side, c], {"gy": to}, MESH)

    def rs_copy(side, u):
        to = jnp.minimum(z + 1, n - 1) if side == 0 else jnp.maximum(z - 1, 0)
        part = pl.ds(u * unit, unit)
        dst = rs_up if side == 0 else rs_dn
        return pltpu.make_async_remote_copy(
            wsum.at[part], dst.at[part], rs_s.at[side, u], rs_r.at[side, u], {"rep": to}, MESH)

    x_sends = (x < nx - 1, x > 0)
    x_gets = (x > 0, x < nx - 1)
    y_sends = (y < ny - 1, y > 0)
    y_gets = (y > 0, y < ny - 1)

    def state(k, rep, r):
        return forcing[rep, r].astype(F32) if k == 0 else states[k - 1, rep, r]

    def forward(i):
        ways = ((up, up_copy, z), (dn, dn_copy, n - 1 - z))
        for buf, copy, hops in ways:
            g = i - ahead * hops
            going = jnp.logical_and(g >= 0, g < STEPS * pieces)

            @pl.when(going)
            def _():
                k, p = lax.div(g, pieces), lax.rem(g, pieces)
                turn, odd = lax.div(p, 2), lax.rem(p, 2)
                c = turn + odd * (pieces - 1 - 2 * turn)
                base = c * per

                @pl.when(hops == 0)
                def _():
                    for r in range(per):
                        buf[k, base + r, 0] = vel[0, base + r]
                        buf[k, base + r, 1] = tra[0, base + r]

                @pl.when(hops > 0)
                def _():
                    copy(k, c).wait_recv()

                @pl.when(jnp.logical_and(hops > 0, hops < n - 1))
                def _():
                    mine = jnp.full((cols, lanes), levels[k], jnp.int32) == z
                    for r in range(per):
                        for part, own in ((0, vel), (1, tra)):
                            got = buf[k, base + r, part].astype(F32)
                            kept = jnp.where(mine, own[0, base + r].astype(F32), got)
                            buf[k, base + r, part] = kept.astype(buf.dtype)

                @pl.when(hops < n - 1)
                def _():
                    copy(k, c).start()

    def unpack(k, c):
        mine = jnp.full((cols, lanes), levels[k], jnp.int32) == z
        below = jnp.full((cols, lanes), levels[k], jnp.int32) < z
        for r in range(c * per, c * per + per):
            speed, tracer = (
                jnp.where(mine, own[0, r].astype(F32),
                          jnp.where(below, up[k, r, part].astype(F32), dn[k, r, part].astype(F32)))
                for part, own in ((0, vel), (1, tra)))
            speed = (0.5 * time_step) * speed
            other = pltpu.roll(speed, half, 1)
            cu[k, r] = jnp.where(first, speed, other)
            cv[k, r] = jnp.where(first, other, speed)
            ct[k, r] = -time_step * tracer

    def flux(k, c):
        for r in range(c * per, c * per + per):
            v_head, v_tail = cv[k, r, 0:1, :], cv[k, r, cols - 1 : cols, :]
            for rep in range(reps):
                s = state(k, rep, r)
                ys[k, 0, r, rep : rep + 1, :] = s[cols - 1 : cols] * (time_step + v_tail)
                ys[k, 1, r, rep : rep + 1, :] = s[0:1] * (time_step - v_head)
        for side in (0, 1):
            @pl.when(y_sends[side])
            def _():
                y_copy(k, side, c).start()
        for side, at, r, sign in ((0, pieces - 1, rows - 1, 1.0), (1, 0, 0, -1.0)):
            if c == at:
                speed = time_step + sign * cu[k, r]
                for rep in range(reps):
                    xs[k, side, rep] = state(k, rep, r) * speed

                @pl.when(x_sends[side])
                def _():
                    x_copy(k, side).start()

    def compute(k, c):
        for side in (0, 1):
            @pl.when(y_gets[side])
            def _():
                y_copy(k, side, c).wait_recv()
        for side, at in ((0, 0), (1, pieces - 1)):
            if c == at:
                @pl.when(x_gets[side])
                def _():
                    x_copy(k, side).wait_recv()
        for r in range(c * per, c * per + per):
            plus = time_step + cv[k, r]
            minus = time_step - cv[k, r]
            trace = ct[k, r]
            sea = ocean[r]
            before = time_step + cu[k, r - 1] if r > 0 else None
            after = time_step - cu[k, r + 1] if r < rows - 1 else None
            total = None
            for rep in range(reps):
                s = state(k, rep, r)
                west = state(k, rep, r - 1) * before if r > 0 else xr[k, 0, rep]
                east = state(k, rep, r + 1) * after if r < rows - 1 else xr[k, 1, rep]
                south = jnp.where(row_of == 0, yr[k, 0, r, rep : rep + 1, :], pltpu.roll(s * plus, 1, 0))
                north = jnp.where(row_of == cols - 1, yr[k, 1, r, rep : rep + 1, :], pltpu.roll(s * minus, cols - 1, 0))
                mixed = trace * s
                mixed = mixed - pltpu.roll(mixed, half, 1)
                new = sea * ((1.0 - 4.0 * time_step) * s + mixed + (west + east) + (south + north))
                if k < STEPS - 1:
                    states[k, rep, r] = new
                else:
                    adj[rep, r] = new
                    term = coef[rep] * new
                    total = term if total is None else total + term
            if k == STEPS - 1:
                wsum[r] = total

    def units_of(c):
        return range(c * per // unit, (c + 1) * per // unit)

    def rs_first(c):
        for u in units_of(c):
            d = u * unit // share
            if d > 0:
                @pl.when(z == 0)
                def _():
                    rs_copy(0, u).start()
            if d < n - 1:
                @pl.when(z == n - 1)
                def _():
                    rs_copy(1, u).start()

    def rs_rest(c):
        for u in units_of(c):
            d = u * unit // share
            part = pl.ds(u * unit, unit)

            @pl.when(jnp.logical_and(z > 0, z < d))
            def _():
                rs_copy(0, u).wait_recv()
                wsum[part] += rs_up[part]
                rs_copy(0, u).start()

            @pl.when(jnp.logical_and(z < n - 1, z > d))
            def _():
                rs_copy(1, u).wait_recv()
                wsum[part] += rs_dn[part]
                rs_copy(1, u).start()

    def rs_last(c):
        for u in units_of(c):
            d = u * unit // share
            part = pl.ds(u * unit, unit)
            here = pl.ds(u * unit - d * share, unit)

            @pl.when(z == d)
            def _():
                if d > 0:
                    rs_copy(0, u).wait_recv()
                if d < n - 1:
                    rs_copy(1, u).wait_recv()
                total = wsum[part]
                if d > 0:
                    total += rs_up[part]
                if d < n - 1:
                    total += rs_dn[part]
                comb[here] = total

    order = []
    for i in range((pieces + 1) // 2):
        order += [i, pieces - 1 - i] if i != pieces - 1 - i else [i]
    ready, have, done = [], set(), set()
    for c in order:
        have.add(c)
        now = [d for d in order if d not in done and all(e in have for e in (d - 1, d, d + 1) if 0 <= e < pieces)]
        done.update(now)
        ready.append(now)

    expected = sum(((at > 0).astype(jnp.int32) + (at < count - 1).astype(jnp.int32)) for _, at, count in links)
    pl.semaphore_wait(barrier, expected)

    schedule = [(k, p) for k in range(STEPS) for p in range(pieces)]
    waiting = []
    lag = ahead * (n - 1)
    for i in range(lag):
        forward(i)
        if i == 0:
            fill_ocean()
            fill_ends()
    for g in range(len(schedule) + 2):
        if g < len(schedule):
            k, p = schedule[g]
            forward(g + lag)
            unpack(k, order[p])
        if g >= 2:
            k, p = schedule[g - 2]
            for c in ready[p]:
                compute(k, c)
                if k == STEPS - 1:
                    rs_first(c)
            if k == STEPS - 1:
                for c in waiting:
                    rs_rest(c)
                waiting = list(ready[p])
        if 1 <= g <= len(schedule):
            k, p = schedule[g - 1]
            flux(k, order[p])
    for c in waiting:
        rs_rest(c)
    for c in order:
        rs_last(c)

    for k in range(STEPS):
        for c in range(pieces):
            @pl.when(z < n - 1)
            def _():
                up_copy(k, c).wait_send()

            @pl.when(z > 0)
            def _():
                dn_copy(k, c).wait_send()

            for side in (0, 1):
                @pl.when(y_sends[side])
                def _():
                    y_copy(k, side, c).wait_send()
        for side in (0, 1):
            @pl.when(x_sends[side])
            def _():
                x_copy(k, side).wait_send()
    for u in range(rows // unit):
        d = u * unit // share

        @pl.when(z < d)
        def _():
            rs_copy(0, u).wait_send()

        @pl.when(z > d)
        def _():
            rs_copy(1, u).wait_send()


def local(sizes, velocity, tracers, forcing, coefficients, land_mask, step_levels):
    n = sizes[0]
    reps, rows, cols, lanes = forcing.shape
    pieces = min(8, rows)
    per, share = rows // pieces, rows // n
    units = rows // min(per, share)
    whole = pl.BlockSpec(memory_space=pltpu.VMEM)
    small = pl.BlockSpec(memory_space=pltpu.SMEM)
    grid = (rows, cols, lanes)
    dma = pltpu.SemaphoreType.DMA
    return pl.pallas_call(
        functools.partial(kernel, sizes, pieces, 2),
        out_shape=(
            jax.ShapeDtypeStruct((share, cols, lanes), F32),
            jax.ShapeDtypeStruct(forcing.shape, F32),
        ),
        in_specs=[whole, whole, whole, small, whole, small],
        out_specs=(whole, whole),
        scratch_shapes=[
            pltpu.VMEM((STEPS - 1, reps) + grid, F32),
            pltpu.VMEM((STEPS, rows, 2, cols, lanes), velocity.dtype),
            pltpu.VMEM((STEPS, rows, 2, cols, lanes), velocity.dtype),
            pltpu.VMEM((STEPS,) + grid, F32),
            pltpu.VMEM((STEPS,) + grid, F32),
            pltpu.VMEM((STEPS,) + grid, F32),
            pltpu.VMEM(grid, F32),
            pltpu.VMEM(grid, F32),
            pltpu.VMEM(grid, F32),
            pltpu.VMEM(grid, F32),
            pltpu.VMEM((STEPS, 2, reps, cols, lanes), F32),
            pltpu.VMEM((STEPS, 2, reps, cols, lanes), F32),
            pltpu.VMEM((STEPS, 2, rows, reps, lanes), F32),
            pltpu.VMEM((STEPS, 2, rows, reps, lanes), F32),
            dma((STEPS, pieces)), dma((STEPS, pieces)),
            dma((STEPS, pieces)), dma((STEPS, pieces)),
            dma((STEPS, 2)), dma((STEPS, 2)),
            dma((STEPS, 2, pieces)), dma((STEPS, 2, pieces)),
            dma((2, units)), dma((2, units)),
        ],
        compiler_params=pltpu.CompilerParams(
            collective_id=0, has_side_effects=True, vmem_limit_bytes=40 * 1024 * 1024
        ),
        cost_estimate=pl.CostEstimate(flops=STEPS * 20 * forcing.size, bytes_accessed=8 * forcing.size, transcendentals=0),
    )(velocity, tracers, forcing, coefficients, land_mask, step_levels)


def solution(mesh):
    placed = (
        P("rep", "gx", "gy", None),
        P("rep", "gx", "gy", None),
        P("rep", "gx", "gy", None),
        P("rep"),
        P("gx", "gy"),
        P(),
    )
    sizes = tuple(mesh.shape[name] for name in ("rep", "gx", "gy"))
    return jax.shard_map(
        functools.partial(local, sizes),
        mesh=mesh,
        in_specs=placed,
        out_specs=(P(("gx", "rep"), "gy", None), P("rep", "gx", "gy", None)),
        check_vma=False,
    )
```

```python
import functools

import jax
import jax.numpy as jnp
from jax import lax
from jax.experimental import pallas as pl
from jax.experimental.pallas import tpu as pltpu
from jax.sharding import PartitionSpec as P

MESH = pl.DeviceIdType.MESH
STEPS = 3
F32 = jnp.float32
time_step = 0.1


def kernel(
    sizes, pieces, ahead, slots,
    vel_h, tra_h, forcing_h, coef_h, mask_h, levels_h,
    comb, adj,
    vel, tra, forcing, coef, mask, levels, in_sem,
    states, up, dn, cu, cv, ct, ocean, wsum, rs_up, rs_dn, xs, xr, ys, yr,
    up_s, up_r, dn_s, dn_r, xs_s, xs_r, ys_s, ys_r, rs_s, rs_r,
):
    n, nx, ny = sizes
    reps, rows, cols, lanes = forcing.shape
    half = lanes // 2
    per = rows // pieces
    share = rows // n
    unit = min(per, share)
    z, x, y = lax.axis_index("rep"), lax.axis_index("gx"), lax.axis_index("gy")

    barrier = pltpu.get_barrier_semaphore()
    links = (("rep", z, n), ("gx", x, nx), ("gy", y, ny))
    for name, at, count in links:
        @pl.when(at > 0)
        def _():
            pl.semaphore_signal(barrier, inc=1, device_id={name: at - 1}, device_id_type=MESH)

        @pl.when(at < count - 1)
        def _():
            pl.semaphore_signal(barrier, inc=1, device_id={name: at + 1}, device_id_type=MESH)

    pairs = ((vel_h, vel), (tra_h, tra), (levels_h, levels), (mask_h, mask), (forcing_h, forcing), (coef_h, coef))
    arrivals = [pltpu.make_async_copy(src, dst, in_sem.at[i]) for i, (src, dst) in enumerate(pairs)]
    for arrival in arrivals:
        arrival.start()

    lane = lax.broadcasted_iota(jnp.int32, (cols, lanes), 1)
    row_of = lax.broadcasted_iota(jnp.int32, (cols, lanes), 0)
    first = lane < half
    eye = lax.broadcasted_iota(jnp.int32, (cols, cols), 0) == lax.broadcasted_iota(jnp.int32, (cols, cols), 1)

    def fill_ocean():
        for r in range(rows):
            line = jnp.where(eye, mask[r : r + 1, :].astype(F32), 0.0)
            ocean[r] = jnp.broadcast_to(jnp.sum(line, axis=1, keepdims=True), (cols, lanes))

    def fill_ends():
        none = jnp.zeros(xr.shape[2:], F32)
        thin = jnp.zeros(yr.shape[2:], F32)
        for k in range(STEPS):
            for side, at, count in ((0, x, 0), (1, x, nx - 1)):
                @pl.when(at == count)
                def _():
                    xr[k, side] = none
            for side, at, count in ((0, y, 0), (1, y, ny - 1)):
                @pl.when(at == count)
                def _():
                    yr[k, side] = thin

    def up_copy(k, c):
        part = up.at[k, pl.ds(c * per, per)]
        return pltpu.make_async_remote_copy(part, part, up_s.at[k, c], up_r.at[k, c], {"rep": jnp.minimum(z + 1, n - 1)}, MESH)

    def dn_copy(k, c):
        part = dn.at[k, pl.ds(c * per, per)]
        return pltpu.make_async_remote_copy(part, part, dn_s.at[k, c], dn_r.at[k, c], {"rep": jnp.maximum(z - 1, 0)}, MESH)

    def x_copy(k, side):
        to = jnp.minimum(x + 1, nx - 1) if side == 0 else jnp.maximum(x - 1, 0)
        return pltpu.make_async_remote_copy(
            xs.at[k, side], xr.at[k, side], xs_s.at[k, side], xs_r.at[k, side], {"gx": to}, MESH)

    def y_copy(k, side, c):
        to = jnp.minimum(y + 1, ny - 1) if side == 0 else jnp.maximum(y - 1, 0)
        part = pl.ds(c * per, per)
        return pltpu.make_async_remote_copy(
            ys.at[k, side, part], yr.at[k, side, part], ys_s.at[k, side, c], ys_r.at[k, side, c], {"gy": to}, MESH)

    def rs_copy(side, u):
        to = jnp.minimum(z + 1, n - 1) if side == 0 else jnp.maximum(z - 1, 0)
        part = pl.ds(u * unit, unit)
        dst = rs_up if side == 0 else rs_dn
        return pltpu.make_async_remote_copy(
            wsum.at[part], dst.at[part], rs_s.at[side, u], rs_r.at[side, u], {"rep": to}, MESH)

    x_sends = (x < nx - 1, x > 0)
    x_gets = (x > 0, x < nx - 1)
    y_sends = (y < ny - 1, y > 0)
    y_gets = (y > 0, y < ny - 1)

    def state(k, rep, r):
        return forcing[rep, r].astype(F32) if k == 0 else states[k - 1, rep, r]

    def level_of(slot):
        if slots == STEPS:
            return levels[slot]
        other = jnp.where(levels[1] == levels[0], levels[2], levels[1])
        return jnp.where(slot == 0, levels[0], other)

    def slot_of(k):
        if slots == STEPS or k == 0:
            return k
        return jnp.where(levels[k] == levels[0], 0, 1)

    def forward(i):
        ways = ((up, up_copy, z), (dn, dn_copy, n - 1 - z))
        for buf, copy, hops in ways:
            g = i - ahead * hops
            going = jnp.logical_and(g >= 0, g < slots * pieces)

            @pl.when(going)
            def _():
                k, p = lax.div(g, pieces), lax.rem(g, pieces)
                turn, odd = lax.div(p, 2), lax.rem(p, 2)
                c = turn + odd * (pieces - 1 - 2 * turn)
                base = c * per

                @pl.when(hops == 0)
                def _():
                    for r in range(per):
                        buf[k, base + r, 0] = vel[0, base + r]
                        buf[k, base + r, 1] = tra[0, base + r]

                @pl.when(hops > 0)
                def _():
                    copy(k, c).wait_recv()

                @pl.when(jnp.logical_and(hops > 0, hops < n - 1))
                def _():
                    mine = jnp.full((cols, lanes), level_of(k), jnp.int32) == z
                    for r in range(per):
                        for part, own in ((0, vel), (1, tra)):
                            got = buf[k, base + r, part].astype(F32)
                            kept = jnp.where(mine, own[0, base + r].astype(F32), got)
                            buf[k, base + r, part] = kept.astype(buf.dtype)

                @pl.when(hops < n - 1)
                def _():
                    copy(k, c).start()

    def unpack(k, c):
        mine = jnp.full((cols, lanes), level_of(k), jnp.int32) == z
        below = jnp.full((cols, lanes), level_of(k), jnp.int32) < z
        for r in range(c * per, c * per + per):
            speed, tracer = (
                jnp.where(mine, own[0, r].astype(F32),
                          jnp.where(below, up[k, r, part].astype(F32), dn[k, r, part].astype(F32)))
                for part, own in ((0, vel), (1, tra)))
            speed = (0.5 * time_step) * speed
            other = pltpu.roll(speed, half, 1)
            cu[k, r] = jnp.where(first, speed, other)
            cv[k, r] = jnp.where(first, other, speed)
            ct[k, r] = -time_step * tracer

    def flux(k, c):
        m = slot_of(k)
        for r in range(c * per, c * per + per):
            v_head, v_tail = cv[m, r, 0:1, :], cv[m, r, cols - 1 : cols, :]
            for rep in range(reps):
                s = state(k, rep, r)
                ys[k, 0, r, rep : rep + 1, :] = s[cols - 1 : cols] * (time_step + v_tail)
                ys[k, 1, r, rep : rep + 1, :] = s[0:1] * (time_step - v_head)
        for side in (0, 1):
            @pl.when(y_sends[side])
            def _():
                y_copy(k, side, c).start()
        for side, at, r, sign in ((0, pieces - 1, rows - 1, 1.0), (1, 0, 0, -1.0)):
            if c == at:
                speed = time_step + sign * cu[m, r]
                for rep in range(reps):
                    xs[k, side, rep] = state(k, rep, r) * speed

                @pl.when(x_sends[side])
                def _():
                    x_copy(k, side).start()

    def compute(k, c):
        m = slot_of(k)
        for side in (0, 1):
            @pl.when(y_gets[side])
            def _():
                y_copy(k, side, c).wait_recv()
        for side, at in ((0, 0), (1, pieces - 1)):
            if c == at:
                @pl.when(x_gets[side])
                def _():
                    x_copy(k, side).wait_recv()
        for r in range(c * per, c * per + per):
            plus = time_step + cv[m, r]
            minus = time_step - cv[m, r]
            trace = ct[m, r]
            sea = ocean[r]
            before = time_step + cu[m, r - 1] if r > 0 else None
            after = time_step - cu[m, r + 1] if r < rows - 1 else None
            total = None
            for rep in range(reps):
                s = state(k, rep, r)
                west = state(k, rep, r - 1) * before if r > 0 else xr[k, 0, rep]
                east = state(k, rep, r + 1) * after if r < rows - 1 else xr[k, 1, rep]
                south = jnp.where(row_of == 0, yr[k, 0, r, rep : rep + 1, :], pltpu.roll(s * plus, 1, 0))
                north = jnp.where(row_of == cols - 1, yr[k, 1, r, rep : rep + 1, :], pltpu.roll(s * minus, cols - 1, 0))
                mixed = trace * s
                mixed = mixed - pltpu.roll(mixed, half, 1)
                new = sea * ((1.0 - 4.0 * time_step) * s + mixed + (west + east) + (south + north))
                if k < STEPS - 1:
                    states[k, rep, r] = new
                else:
                    adj[rep, r] = new
                    term = coef[rep] * new
                    total = term if total is None else total + term
            if k == STEPS - 1:
                wsum[r] = total

    def units_of(c):
        return range(c * per // unit, (c + 1) * per // unit)

    def rs_first(c):
        for u in units_of(c):
            d = u * unit // share
            if d > 0:
                @pl.when(z == 0)
                def _():
                    rs_copy(0, u).start()
            if d < n - 1:
                @pl.when(z == n - 1)
                def _():
                    rs_copy(1, u).start()

    def rs_rest(c):
        for u in units_of(c):
            d = u * unit // share
            part = pl.ds(u * unit, unit)

            @pl.when(jnp.logical_and(z > 0, z < d))
            def _():
                rs_copy(0, u).wait_recv()
                wsum[part] += rs_up[part]
                rs_copy(0, u).start()

            @pl.when(jnp.logical_and(z < n - 1, z > d))
            def _():
                rs_copy(1, u).wait_recv()
                wsum[part] += rs_dn[part]
                rs_copy(1, u).start()

    def rs_last(c):
        for u in units_of(c):
            d = u * unit // share
            part = pl.ds(u * unit, unit)
            here = pl.ds(u * unit - d * share, unit)

            @pl.when(z == d)
            def _():
                if d > 0:
                    rs_copy(0, u).wait_recv()
                if d < n - 1:
                    rs_copy(1, u).wait_recv()
                total = wsum[part]
                if d > 0:
                    total += rs_up[part]
                if d < n - 1:
                    total += rs_dn[part]
                comb[here] = total

    order = []
    for i in range((pieces + 1) // 2):
        order += [i, pieces - 1 - i] if i != pieces - 1 - i else [i]
    ready, have, done = [], set(), set()
    for c in order:
        have.add(c)
        now = [d for d in order if d not in done and all(e in have for e in (d - 1, d, d + 1) if 0 <= e < pieces)]
        done.update(now)
        ready.append(now)

    expected = sum(((at > 0).astype(jnp.int32) + (at < count - 1).astype(jnp.int32)) for _, at, count in links)
    for arrival in arrivals:
        arrival.wait()
    pl.semaphore_wait(barrier, expected)

    lag = ahead * (n - 1)
    arrived, turn, waiting = 0, 0, []
    fluxed, computed = [0] * STEPS, [0] * STEPS
    while computed[-1] < pieces:
        if turn < lag + slots * pieces:
            forward(turn)
            most = 2
        else:
            most = pieces // 2
        if turn == 0:
            fill_ocean()
            fill_ends()
        if lag <= turn < lag + slots * pieces:
            unpack(arrived // pieces, order[arrived % pieces])
            arrived += 1
        left, sent = most, list(fluxed)
        for k in range(STEPS):
            while left and computed[k] < sent[k]:
                for c in ready[computed[k]]:
                    compute(k, c)
                    if k == STEPS - 1:
                        rs_first(c)
                if k == STEPS - 1:
                    for c in waiting:
                        rs_rest(c)
                    waiting = list(ready[computed[k]])
                computed[k] += 1
                left -= 1
        left = most
        for k in range(STEPS):
            known = arrived - min(k, slots - 1) * pieces - (1 if arrived < slots * pieces else 0)
            while left and fluxed[k] < min(pieces, known):
                c = order[fluxed[k]]
                if k > 0 and not any(c in ready[p] for p in range(computed[k - 1])):
                    break
                flux(k, c)
                fluxed[k] += 1
                left -= 1
        turn += 1
    for c in waiting:
        rs_rest(c)
    for c in order:
        rs_last(c)

    for k in range(slots):
        for c in range(pieces):
            @pl.when(z < n - 1)
            def _():
                up_copy(k, c).wait_send()

            @pl.when(z > 0)
            def _():
                dn_copy(k, c).wait_send()

    for k in range(STEPS):
        for c in range(pieces):
            for side in (0, 1):
                @pl.when(y_sends[side])
                def _():
                    y_copy(k, side, c).wait_send()
        for side in (0, 1):
            @pl.when(x_sends[side])
            def _():
                x_copy(k, side).wait_send()
    for u in range(rows // unit):
        d = u * unit // share

        @pl.when(z < d)
        def _():
            rs_copy(0, u).wait_send()

        @pl.when(z > d)
        def _():
            rs_copy(1, u).wait_send()


def sweep(sizes, slots, velocity, tracers, forcing, coefficients, land_mask, step_levels):
    n = sizes[0]
    reps, rows, cols, lanes = forcing.shape
    pieces = min(8, rows)
    per, share = rows // pieces, rows // n
    units = rows // min(per, share)
    whole = pl.BlockSpec(memory_space=pltpu.VMEM)
    far = pl.BlockSpec(memory_space=pltpu.HBM)
    grid = (rows, cols, lanes)
    dma = pltpu.SemaphoreType.DMA
    return pl.pallas_call(
        functools.partial(kernel, sizes, pieces, 3, slots),
        out_shape=(
            jax.ShapeDtypeStruct((share, cols, lanes), F32),
            jax.ShapeDtypeStruct(forcing.shape, F32),
        ),
        in_specs=[far] * 6,
        out_specs=(whole, whole),
        scratch_shapes=[
            pltpu.VMEM(velocity.shape, velocity.dtype),
            pltpu.VMEM(tracers.shape, tracers.dtype),
            pltpu.VMEM(forcing.shape, forcing.dtype),
            pltpu.SMEM(coefficients.shape, coefficients.dtype),
            pltpu.VMEM(land_mask.shape, land_mask.dtype),
            pltpu.SMEM(step_levels.shape, step_levels.dtype),
            dma((6,)),
            pltpu.VMEM((STEPS - 1, reps) + grid, F32),
            pltpu.VMEM((slots, rows, 2, cols, lanes), velocity.dtype),
            pltpu.VMEM((slots, rows, 2, cols, lanes), velocity.dtype),
            pltpu.VMEM((slots,) + grid, F32),
            pltpu.VMEM((slots,) + grid, F32),
            pltpu.VMEM((slots,) + grid, F32),
            pltpu.VMEM(grid, F32),
            pltpu.VMEM(grid, F32),
            pltpu.VMEM(grid, F32),
            pltpu.VMEM(grid, F32),
            pltpu.VMEM((STEPS, 2, reps, cols, lanes), F32),
            pltpu.VMEM((STEPS, 2, reps, cols, lanes), F32),
            pltpu.VMEM((STEPS, 2, rows, reps, lanes), F32),
            pltpu.VMEM((STEPS, 2, rows, reps, lanes), F32),
            dma((slots, pieces)), dma((slots, pieces)),
            dma((slots, pieces)), dma((slots, pieces)),
            dma((STEPS, 2)), dma((STEPS, 2)),
            dma((STEPS, 2, pieces)), dma((STEPS, 2, pieces)),
            dma((2, units)), dma((2, units)),
        ],
        compiler_params=pltpu.CompilerParams(
            collective_id=slots, has_side_effects=True, vmem_limit_bytes=63 * 1024 * 1024
        ),
        cost_estimate=pl.CostEstimate(flops=STEPS * 20 * forcing.size, bytes_accessed=8 * forcing.size, transcendentals=0),
    )(velocity, tracers, forcing, coefficients, land_mask, step_levels)


def local(sizes, *args):
    a, b, c = args[-1][0], args[-1][1], args[-1][2]
    apart = (a != b) & (a != c) & (b != c)
    return lax.cond(
        apart, functools.partial(sweep, sizes, STEPS), functools.partial(sweep, sizes, STEPS - 1), *args)


def solution(mesh):
    placed = (
        P("rep", "gx", "gy", None),
        P("rep", "gx", "gy", None),
        P("rep", "gx", "gy", None),
        P("rep"),
        P("gx", "gy"),
        P(),
    )
    sizes = tuple(mesh.shape[name] for name in ("rep", "gx", "gy"))
    return jax.shard_map(
        functools.partial(local, sizes),
        mesh=mesh,
        in_specs=placed,
        out_specs=(P(("gx", "rep"), "gy", None), P("rep", "gx", "gy", None)),
        check_vma=False,
    )
```
